32 devices in a mesh: seq: 16 (over z, x, core), ctx: 2 (over y).
Axes of the slice: x: 2, y: 2, z: 4, core: 2. Of those that a mesh axis runs over, the one named last changes fastest.
Arguments:
- tokens: bfloat16 [16384, 1024], P(('seq', 'ctx')), may hold values from -6 to 6
- segments: int32 [16, 1024], P('seq'), may hold values from 0 to 2, as said below
- cotangent: bfloat16 [16384, 1024], P(('seq', 'ctx')), may hold values from -6 to 6
- w_query: bfloat16 [1024, 1024], P(('seq', 'ctx')), may hold values from -0.1875 to 0.1875
- b_query: bfloat16 [1024], P(('seq', 'ctx')), may hold values from -1.1953125 to 1.1953125
- w_key: bfloat16 [1024, 1024], P(('seq', 'ctx')), may hold values from -0.1875 to 0.1875
- w_value: bfloat16 [1024, 1024], P(('seq', 'ctx')), may hold values from -0.1875 to 0.1875
- b_value: bfloat16 [1024], P(('seq', 'ctx')), may hold values from -0.29882812 to 0.29882812
- w_output: bfloat16 [1024, 1024], P(('seq', 'ctx')), may hold values from -3 to 3
- b_output: bfloat16 [1024], P(('seq', 'ctx')), may hold values from -0.59765625 to 0.59765625
- gain_attn: bfloat16 [1024], P(('seq', 'ctx')), may hold values from 0.5 to 1.5
- shift_attn: bfloat16 [1024], P(('seq', 'ctx')), may hold values from -0.59765625 to 0.59765625
- w_inner: bfloat16 [1024, 4096], P(('seq', 'ctx')), may hold values from -0.1875 to 0.1875
- b_inner: bfloat16 [4096], P(('seq', 'ctx')), may hold values from -1.1953125 to 1.1953125
- w_outer: bfloat16 [4096, 1024], P(('seq', 'ctx')), may hold values from -0.09375 to 0.09375
- b_outer: bfloat16 [1024], P(('seq', 'ctx')), may hold values from -0.59765625 to 0.59765625
- gain_ffn: bfloat16 [1024], P(('seq', 'ctx')), may hold values from 0.5 to 1.5
- shift_ffn: bfloat16 [1024], P(('seq', 'ctx')), may hold values from -0.59765625 to 0.59765625
Outputs:
- out_tokens: bfloat16 [16384, 1024], P(('seq', 'ctx'))
- grad_tokens: float32 [16384, 1024], P(('seq', 'ctx'))
- grad_wquery: float32 [1024, 1024], P(('seq', 'ctx'))
- grad_bquery: float32 [1024], P(('seq', 'ctx'))
- grad_wkey: float32 [1024, 1024], P(('seq', 'ctx'))
- grad_wvalue: float32 [1024, 1024], P(('seq', 'ctx'))
- grad_bvalue: float32 [1024], P(('seq', 'ctx'))
- grad_woutput: float32 [1024, 1024], P(('seq', 'ctx'))
- grad_boutput: float32 [1024], P(('seq', 'ctx'))
- grad_gattn: float32 [1024], P(('seq', 'ctx'))
- grad_sattn: float32 [1024], P(('seq', 'ctx'))
- grad_winner: float32 [1024, 4096], P(('seq', 'ctx'))
- grad_binner: float32 [4096], P(('seq', 'ctx'))
- grad_wouter: float32 [4096, 1024], P(('seq', 'ctx'))
- grad_bouter: float32 [1024], P(('seq', 'ctx'))
- grad_gffn: float32 [1024], P(('seq', 'ctx'))
- grad_sffn: float32 [1024], P(('seq', 'ctx'))
The draws below stay inside these ranges and needn't reach their ends.
Inputs may be any that keep to these rules, and one draw needn't show every extreme that they name: `segments`: each row is one sequence. Segment numbers never fall, start at 0 and end at 2 in every row; segment 1 begins within the first 512 positions and ends within the last 512.
All inputs are finite; a program needn't handle non-finite values.
Results may differ from the reference program's by a relative error of at most 0.015.
Values may be sent and summed in bfloat16 or wider, within the bound.
A program may use at most 192 MiB of HBM per device.

```python
import jax
import jax.numpy as jnp
from jax import lax

D = 1024
HEADS = 16
HEAD_DIM = 64
FF = 4096
SEQ_LEN = 1024
TOK_DEV = 512
SEQS = 16
TOKENS = 16384


def draw_segments(key, part):
    key = jax.random.fold_in(key, 11)
    head_key, tail_key = jax.random.split(key)
    head_len = jax.random.randint(head_key, (SEQS, 1), 1, TOK_DEV)
    tail_len = jax.random.randint(tail_key, (SEQS, 1), 1, TOK_DEV)
    position = jnp.arange(SEQ_LEN, dtype=jnp.int32)[None, :]
    first = (position >= head_len).astype(jnp.int32)
    second = (position >= SEQ_LEN - tail_len).astype(jnp.int32)
    return first + second


def level_of(key, extent, pieces, smallest, largest):
    level = 1.0
    for dim, parts in pieces:
        steps = jax.random.uniform(jax.random.fold_in(jax.random.fold_in(key, 6), dim), (parts,), jnp.float32, smallest / len(pieces), largest / len(pieces))
        level = level * jnp.repeat(jnp.exp(steps), extent[dim] // parts).reshape((-1,) + (1,) * (len(extent) - 1 - dim))
    return level


def bell_draw(key, shape, deviation, limit, pieces=(), held_as=jnp.bfloat16):
    values = jax.random.normal(key, shape, jnp.float32) * deviation
    if len(pieces) > 0:
        values = level_of(key, shape, pieces, -0.22, 0.18) * values
    return jnp.clip(values, min=-limit, max=limit).astype(held_as)


def setup_inputs(seed: int = 0) -> dict:
    splits = jax.random.split(jax.random.key(seed), 19)
    tokens = bell_draw(splits[0], (TOKENS, D), 1.0, 6.0, ((0, 32),))
    segments = draw_segments(jax.random.fold_in(splits[18], 71), 0)
    cotangent = bell_draw(splits[2], (TOKENS, D), 1.0, 6.0, ((0, 32),))
    w_query = bell_draw(splits[3], (D, D), D ** -0.5, 0.1875, ((0, 32),))
    b_query = bell_draw(splits[4], (D,), 0.2, 1.1953125, ((0, 32),))
    w_key = bell_draw(splits[5], (D, D), D ** -0.5, 0.1875, ((0, 32),))
    w_value = bell_draw(splits[6], (D, D), D ** -0.5, 0.1875, ((0, 32),))
    b_value = bell_draw(splits[7], (D,), 0.05, 0.29882812, ((0, 32),))
    w_output = bell_draw(splits[8], (D, D), (max(D // 256, 1)) ** -0.5, 3.0, ((0, 32),))
    b_output = bell_draw(splits[9], (D,), 0.1, 0.59765625, ((0, 32),))
    gain_attn = jnp.clip(1.0 + 0.1 * jax.random.normal(splits[10], (D,), jnp.float32), 0.5, 1.5).astype(jnp.bfloat16)
    shift_attn = bell_draw(splits[11], (D,), 0.1, 0.59765625, ((0, 32),))
    w_inner = bell_draw(splits[12], (D, FF), D ** -0.5, 0.1875, ((0, 32),))
    b_inner = bell_draw(splits[13], (FF,), 0.2, 1.1953125, ((0, 32),))
    w_outer = bell_draw(splits[14], (FF, D), FF ** -0.5, 0.09375, ((0, 32),))
    b_outer = bell_draw(splits[15], (D,), 0.1, 0.59765625, ((0, 32),))
    gain_ffn = jnp.clip(1.0 + 0.1 * jax.random.normal(splits[16], (D,), jnp.float32), 0.5, 1.5).astype(jnp.bfloat16)
    shift_ffn = bell_draw(splits[17], (D,), 0.1, 0.59765625, ((0, 32),))
    return dict(tokens=tokens, segments=segments, cotangent=cotangent, w_query=w_query, b_query=b_query, w_key=w_key, w_value=w_value, b_value=b_value, w_output=w_output, b_output=b_output, gain_attn=gain_attn, shift_attn=shift_attn, w_inner=w_inner, b_inner=b_inner, w_outer=w_outer, b_outer=b_outer, gain_ffn=gain_ffn, shift_ffn=shift_ffn)


@jax.custom_vjp
def low(v):
    return lax.optimization_barrier(v.astype(jnp.bfloat16)).astype(jnp.float32)

@jax.custom_vjp
def low_back(v):
    return v

def low_keep(v):
    return (low(v), None)

def low_pass(kept, grad):
    return (grad,)

def back_keep(v):
    return (v, None)

def back_low(kept, grad):
    return (low(grad),)
low.defvjp(low_keep, low_pass)
low_back.defvjp(back_keep, back_low)

def matmul(left, right):
    return jnp.dot(left, right, precision=lax.Precision.HIGHEST)

def layer_norm(z, gain, shift):
    center = z - lax.optimization_barrier(jnp.mean(z, axis=-1, keepdims=True))
    spread = lax.optimization_barrier(jnp.mean(center * center, axis=-1, keepdims=True))
    return center * lax.rsqrt(spread + 1e-05) * gain + shift

def attend_one(item):
    queries, keys, values, labels = item
    scores = low_back(jnp.einsum('qhd,khd->hqk', queries, keys, precision=lax.Precision.HIGHEST) * 0.125)
    allowed = (labels[:, None] == labels[None, :])[None]
    masked = jnp.where(allowed, scores, -1000000000.0)
    probs = jax.nn.softmax(masked, axis=-1)
    return jnp.einsum('hqk,khd->qhd', low(probs), values, precision=lax.Precision.HIGHEST)

def layer(x, wq, bq, wk, wv, bv, wo, bo, ga, sa, wi, bi, wu, bu, gf, sf, segments):
    queries = low_back(low(matmul(x, wq) + bq))
    keys = low_back(low(matmul(x, wk)))
    values = low_back(low(matmul(x, wv) + bv))
    shape = (SEQS, SEQ_LEN, HEADS, HEAD_DIM)
    mixed = lax.map(jax.checkpoint(attend_one), (queries.reshape(shape), keys.reshape(shape), values.reshape(shape), segments))
    attended = low_back(low(mixed.reshape(TOKENS, D)))
    branch_one = low_back(matmul(attended, wo) + bo)
    normed_one = layer_norm(x + branch_one, ga, sa)
    inner = low_back(matmul(low(normed_one), wi) + bi)
    branch_two = low_back(matmul(low(jax.nn.gelu(inner, approximate=False)), wu) + bu)
    return layer_norm(normed_one + branch_two, gf, sf)

def reference(tokens, segments, cotangent, w_query, b_query, w_key, w_value, b_value, w_output, b_output, gain_attn, shift_attn, w_inner, b_inner, w_outer, b_outer, gain_ffn, shift_ffn):
    params = (w_query, b_query, w_key, w_value, b_value, w_output, b_output, gain_attn, shift_attn, w_inner, b_inner, w_outer, b_outer, gain_ffn, shift_ffn)
    params = tuple((p.astype(jnp.float32) for p in params))

    def forward(x, *weights):
        return layer(x, *weights, segments)
    result, pull = jax.vjp(forward, tokens.astype(jnp.float32), *params)
    grads = pull(cotangent.astype(jnp.float32))
    return (result.astype(jnp.bfloat16), grads[0], grads[1], grads[2], grads[3], grads[4], grads[5], grads[6], grads[7], grads[8], grads[9], grads[10], grads[11], grads[12], grads[13], grads[14], grads[15])
```

```python
import functools

import jax
import jax.numpy as jnp
from jax import lax
from jax.experimental import pallas as pl
from jax.experimental.pallas import tpu as pltpu
from jax.sharding import PartitionSpec as P

HEAD_DIM = 64
BOTH = ("seq", "ctx")
F32 = jnp.float32
BF16 = jnp.bfloat16


def layer_norm(z, gain, shift):
    center = z - jnp.mean(z, axis=-1, keepdims=True)
    spread = jnp.mean(center * center, axis=-1, keepdims=True)
    return center * lax.rsqrt(spread + 1e-05) * gain + shift


def exact_gelu(value):
    return jax.nn.gelu(value, approximate=False)


def matmul_tn(left, right):
    return lax.dot_general(
        left, right, (((0,), (0,)), ((), ())), preferred_element_type=F32
    )


def matmul_nt(left, right):
    return lax.dot_general(
        left, right, (((1,), (1,)), ((), ())), preferred_element_type=F32
    )


def head_part(array, index):
    lane = lax.broadcasted_iota(jnp.int32, array.shape, 1)
    inside = (lane >= index * HEAD_DIM) & (lane < (index + 1) * HEAD_DIM)
    return jnp.where(inside, array, jnp.zeros_like(array))


def probs_of(queries, keys, allowed):
    masked = jnp.where(allowed, matmul_nt(queries, keys), -1000000000.0)
    expo = jnp.exp(masked - jnp.max(masked, axis=-1, keepdims=True))
    return expo * (1.0 / jnp.sum(expo, axis=-1, keepdims=True))


def attend_kernel(q_ref, k_ref, v_ref, col_ref, row_ref, out_ref):
    allowed = col_ref[...] == row_ref[...]
    queries = q_ref[...] * jnp.asarray(0.125, BF16)
    total = jnp.zeros(out_ref.shape, F32)
    for index in range(2):
        probs = probs_of(queries, head_part(k_ref[...], index), allowed).astype(BF16)
        total += jnp.dot(probs, head_part(v_ref[...], index), preferred_element_type=F32)
    out_ref[...] = total.astype(BF16)


def attend_back_kernel(
    q_ref, k_ref, v_ref, g_ref, col_ref, row_ref, dq_ref, dk_ref, dv_ref, dk_sum, dv_sum
):
    step = pl.program_id(1)
    allowed = col_ref[...] == row_ref[...]
    queries = q_ref[...] * jnp.asarray(0.125, BF16)
    grads = g_ref[...]

    @pl.when(step == 0)
    def _():
        dk_sum[...] = jnp.zeros_like(dk_sum)
        dv_sum[...] = jnp.zeros_like(dv_sum)

    dq = jnp.zeros(dq_ref.shape, F32)
    for index in range(2):
        keys = head_part(k_ref[...], index)
        probs = probs_of(queries, keys, allowed)
        d_probs = matmul_nt(grads, head_part(v_ref[...], index))
        inner = jnp.sum(d_probs * probs, axis=-1, keepdims=True)
        scores_low = (probs * (d_probs - inner)).astype(BF16)
        dq += jnp.dot(scores_low, keys, preferred_element_type=F32)
        dk_sum[...] += matmul_tn(scores_low, head_part(queries, index))
        dv_sum[...] += matmul_tn(probs.astype(BF16), head_part(grads, index))
    dq_ref[...] = (dq * 0.125).astype(BF16)

    @pl.when(step == pl.num_programs(1) - 1)
    def _():
        dk_ref[...] = dk_sum[...].astype(BF16)
        dv_ref[...] = dv_sum[...].astype(BF16)


def attention_specs(length, pairs, block):
    rows = pl.BlockSpec((block, 128), lambda p, i: (i, p))

    def whole(third):
        return pl.BlockSpec((length, 128), lambda p, i: (0, p + third * pairs))

    labels = [
        pl.BlockSpec((block, 1), lambda p, i: (i, 0)),
        pl.BlockSpec((1, length), lambda p, i: (0, 0)),
    ]
    return rows, whole, labels


def attend(qkv, column, row):
    length = qkv.shape[0]
    width = qkv.shape[1] // 3
    pairs, block = width // 128, 256
    rows, whole, labels = attention_specs(length, pairs, block)
    return pl.pallas_call(
        attend_kernel,
        grid=(pairs, length // block),
        in_specs=[rows, whole(1), whole(2)] + labels,
        out_specs=rows,
        out_shape=jax.ShapeDtypeStruct((length, width), BF16),
        compiler_params=pltpu.CompilerParams(vmem_limit_bytes=40 << 20),
        cost_estimate=pl.CostEstimate(
            flops=60 * length * length * width, bytes_accessed=8 * length * width, transcendentals=0
        ),
    )(qkv, qkv, qkv, column, row)


def attend_back(qkv, grads, column, row):
    length = qkv.shape[0]
    width = qkv.shape[1] // 3
    pairs, block = width // 128, 256
    rows, whole, labels = attention_specs(length, pairs, block)
    out = jax.ShapeDtypeStruct((length, width), BF16)
    return pl.pallas_call(
        attend_back_kernel,
        grid=(pairs, length // block),
        in_specs=[rows, whole(1), whole(2), rows] + labels,
        out_specs=[rows, whole(0), whole(0)],
        out_shape=[out, out, out],
        scratch_shapes=[pltpu.VMEM((length, 128), F32), pltpu.VMEM((length, 128), F32)],
        compiler_params=pltpu.CompilerParams(vmem_limit_bytes=48 << 20),
        cost_estimate=pl.CostEstimate(
            flops=130 * length * length * width,
            bytes_accessed=14 * length * width,
            transcendentals=0,
        ),
    )(qkv, qkv, qkv, grads, column, row)


def swap(stacked):
    count = stacked.shape[0]
    if count != 2:
        return lax.all_to_all(stacked, "ctx", 0, 0)
    place = lax.axis_index("ctx")
    mine = lax.dynamic_index_in_dim(stacked, place, 0, keepdims=False)
    sent = lax.dynamic_index_in_dim(stacked, 1 - place, 0, keepdims=False)
    got = lax.ppermute(sent, "ctx", [(0, 1), (1, 0)])
    first = place == 0
    return jnp.stack([jnp.where(first, mine, got), jnp.where(first, got, mine)])


def gather_ctx(array, count):
    if count != 2:
        return lax.all_gather(array, "ctx", axis=0, tiled=True)
    got = lax.ppermute(array, "ctx", [(0, 1), (1, 0)])
    first = lax.axis_index("ctx") == 0
    return jnp.concatenate([jnp.where(first, array, got), jnp.where(first, got, array)], axis=0)


def split_sum(value):
    high = value.astype(BF16)
    return high, (value - high.astype(F32)).astype(BF16)


def per_device(
    tokens,
    segments,
    cotangent,
    w_query,
    b_query,
    w_key,
    w_value,
    b_value,
    w_output,
    b_output,
    gain_attn,
    shift_attn,
    w_inner,
    b_inner,
    w_outer,
    b_outer,
    gain_ffn,
    shift_ffn,
):
    rows, width = tokens.shape
    seq_count = lax.axis_size("seq")
    ctx_count = lax.axis_size("ctx")
    count = seq_count * ctx_count
    place = lax.axis_index("ctx")
    part = width // ctx_count
    own = w_query.shape[0]
    wide = b_inner.shape[0]
    labels = segments[0]
    column, row = labels[:, None], labels[None, :]

    vectors = jnp.concatenate(
        [b_query, b_value, b_output, gain_attn, shift_attn, b_outer, gain_ffn, shift_ffn, b_inner]
    )
    extra = jnp.pad(vectors[None, :], ((0, 15), (0, width - vectors.shape[0])))
    packed = jnp.concatenate([w_query, w_key, w_value, w_output, extra], axis=0)
    gathered = lax.all_gather(packed, BOTH, axis=0, tiled=False)
    tokens_all = gather_ctx(tokens, ctx_count)
    winner = lax.all_gather(w_inner, BOTH, axis=0, tiled=True)
    wouter = lax.all_gather(w_outer, BOTH, axis=0, tiled=True)

    wquery, wkey, wvalue, woutput = (
        gathered[:, i * own : (i + 1) * own].reshape(width, width) for i in range(4)
    )
    small = gathered[:, 4 * own].astype(F32)
    bquery, bvalue, boutput, gattn, sattn, bouter, gffn, sffn = (
        small[:, i * own : (i + 1) * own].reshape(width) for i in range(8)
    )
    binner = small[:, 8 * own : 8 * own + wide].reshape(-1)

    def my_cols(array):
        return lax.dynamic_slice_in_dim(array, place * part, part, array.ndim - 1)

    w_three = jnp.concatenate([my_cols(wquery), my_cols(wkey), my_cols(wvalue)], axis=1)
    b_three = jnp.concatenate([my_cols(bquery), jnp.zeros((part,), F32), my_cols(bvalue)])
    qkv = (jnp.dot(tokens_all, w_three, preferred_element_type=F32) + b_three).astype(BF16)
    mixed = attend(qkv, column, row)
    mixed = swap(mixed.reshape(ctx_count, rows, part))
    attended = jnp.transpose(mixed, (1, 0, 2)).reshape(rows, width)

    pre_one = (
        tokens.astype(F32) + jnp.dot(attended, woutput, preferred_element_type=F32) + boutput
    )
    normed_one = layer_norm(pre_one, gattn, sattn)
    normed_low = normed_one.astype(BF16)
    inner = jnp.dot(normed_low, winner, preferred_element_type=F32) + binner
    act_low = exact_gelu(inner).astype(BF16)
    pre_two = normed_one + jnp.dot(act_low, wouter, preferred_element_type=F32) + bouter
    out_value = layer_norm(pre_two, gffn, sffn)

    grad_out = cotangent.astype(F32)
    _, norm_two_back = jax.vjp(layer_norm, pre_two, gffn, sffn)
    d_pre_two, d_gain_two, d_shift_two = norm_two_back(grad_out)
    outer_low = d_pre_two.astype(BF16)
    grad_bouter = jnp.sum(outer_low.astype(F32), axis=0)
    part_wouter = matmul_tn(act_low, outer_low).astype(BF16)
    out_wouter = lax.psum_scatter(part_wouter, BOTH, scatter_dimension=0, tiled=True)
    d_act = matmul_nt(outer_low, wouter)
    _, gelu_back = jax.vjp(exact_gelu, inner)
    inner_low = gelu_back(d_act)[0].astype(BF16)
    grad_binner = jnp.sum(inner_low.astype(F32), axis=0)
    part_winner = matmul_tn(normed_low, inner_low).astype(BF16)
    out_winner = lax.psum_scatter(part_winner, BOTH, scatter_dimension=0, tiled=True)
    d_normed = d_pre_two + matmul_nt(inner_low, winner)

    _, norm_one_back = jax.vjp(layer_norm, pre_one, gattn, sattn)
    d_pre_one, d_gain_one, d_shift_one = norm_one_back(d_normed)
    out_low = d_pre_one.astype(BF16)
    grad_boutput = jnp.sum(out_low.astype(F32), axis=0)
    d_attended = matmul_nt(out_low, woutput).astype(BF16)
    d_mixed = swap(jnp.transpose(d_attended.reshape(rows, ctx_count, part), (1, 0, 2)))
    d_mixed = d_mixed.reshape(ctx_count * rows, part)

    part_woutput = matmul_tn(attended, out_low).astype(BF16)
    sums = jnp.concatenate(
        [
            v.reshape(count, -1)
            for v in (
                grad_boutput, d_gain_one, d_shift_one, grad_bouter, d_gain_two, d_shift_two,
                grad_binner,
            )
        ],
        axis=1,
    )
    high, low = split_sum(sums)
    used = sums.shape[1]
    tail = jnp.pad(
        jnp.concatenate([high, low], axis=1)[:, None, :], ((0, 0), (0, 15), (0, width - 2 * used))
    )
    block = jnp.concatenate([part_woutput.reshape(count, own, width), tail], axis=1)
    block = lax.psum_scatter(block, BOTH, scatter_dimension=0, tiled=False)
    out_woutput = block[:own].astype(F32)
    sums = (block[own, :used].astype(F32) + block[own, used : 2 * used].astype(F32))
    out_boutput, out_gattn, out_sattn, out_bouter, out_gffn, out_sffn = (
        sums[i * own : (i + 1) * own] for i in range(6)
    )
    out_binner = sums[6 * own :]

    d_query, d_key, d_value = attend_back(qkv, d_mixed, column, row)
    d_three = jnp.concatenate([d_query, d_key, d_value], axis=1)

    part_three = matmul_tn(tokens_all, d_three).astype(BF16)
    bias = jnp.sum(d_three.astype(F32), axis=0)

    def spread(vector):
        whole = jnp.zeros((width,), F32)
        whole = lax.dynamic_update_slice_in_dim(whole, vector, place * part, 0)
        return whole.reshape(seq_count, ctx_count, own)

    pair = jnp.concatenate([spread(bias[:part]), spread(bias[2 * part :])], axis=2)
    high, low = split_sum(pair)
    tail = jnp.pad(
        jnp.concatenate([high, low], axis=2)[:, :, None, :],
        ((0, 0), (0, 0), (0, 15), (0, 3 * part - 4 * own)),
    )
    block = jnp.concatenate(
        [part_three.reshape(seq_count, ctx_count, own, 3 * part), tail], axis=2
    )
    block = lax.psum_scatter(block, "seq", scatter_dimension=0, tiled=False)

    d_part = matmul_nt(d_three, w_three)
    got = swap(d_part.astype(BF16).reshape(ctx_count, rows, width))
    grad_tokens = d_pre_one + jnp.sum(got.astype(F32), axis=0)

    block = swap(block).astype(F32)
    out_wquery, out_wkey, out_wvalue = (
        jnp.transpose(block[:, :own, i * part : (i + 1) * part], (1, 0, 2)).reshape(own, width)
        for i in range(3)
    )
    pair = jnp.sum(block[:, own], axis=0)
    pair = pair[: 2 * own] + pair[2 * own : 4 * own]
    out_bquery, out_bvalue = pair[:own], pair[own:]
    return (
        out_value.astype(BF16),
        grad_tokens,
        out_wquery,
        out_bquery,
        out_wkey,
        out_wvalue,
        out_bvalue,
        out_woutput,
        out_boutput,
        out_gattn,
        out_sattn,
        out_winner.astype(F32),
        out_binner,
        out_wouter.astype(F32),
        out_bouter,
        out_gffn,
        out_sffn,
    )


def solution(mesh):
    matrix, vector = P(BOTH, None), P(BOTH)
    return jax.shard_map(
        per_device,
        mesh=mesh,
        in_specs=(
            matrix, P("seq", None), matrix, matrix, vector, matrix, matrix, vector, matrix,
            vector, vector, vector, matrix, vector, matrix, vector, vector, vector,
        ),
        out_specs=(
            matrix, matrix, matrix, vector, matrix, matrix, vector, matrix, vector, vector,
            vector, matrix, vector, matrix, vector, vector, vector,
        ),
        check_vma=False,
    )
```

```python
import jax
import jax.numpy as jnp
from jax import lax
from jax.experimental import pallas as pl
from jax.experimental.pallas import tpu as pltpu
from jax.sharding import PartitionSpec as P

HEAD_DIM = 64
BOTH = ("seq", "ctx")
F32 = jnp.float32
BF16 = jnp.bfloat16


def layer_norm(z, gain, shift):
    center = z - jnp.mean(z, axis=-1, keepdims=True)
    spread = jnp.mean(center * center, axis=-1, keepdims=True)
    return center * lax.rsqrt(spread + 1e-05) * gain + shift


def exact_gelu(value):
    return jax.nn.gelu(value, approximate=False)


def matmul_tn(left, right):
    return lax.dot_general(
        left, right, (((0,), (0,)), ((), ())), preferred_element_type=F32
    )


def matmul_nt(left, right):
    return lax.dot_general(
        left, right, (((1,), (1,)), ((), ())), preferred_element_type=F32
    )


def head_part(array, index):
    lane = lax.broadcasted_iota(jnp.int32, array.shape, 1)
    inside = (lane >= index * HEAD_DIM) & (lane < (index + 1) * HEAD_DIM)
    return jnp.where(inside, array, jnp.zeros_like(array))


def probs_of(queries, keys, allowed):
    masked = jnp.where(allowed, matmul_nt(queries, keys), -1000000000.0)
    expo = jnp.exp(masked - jnp.max(masked, axis=-1, keepdims=True))
    return expo * (1.0 / jnp.sum(expo, axis=-1, keepdims=True))


def attend_kernel(q_ref, k_ref, v_ref, col_ref, row_ref, out_ref):
    allowed = col_ref[...] == row_ref[...]
    queries = q_ref[...] * jnp.asarray(0.125, BF16)
    total = jnp.zeros(out_ref.shape, F32)
    for index in range(2):
        probs = probs_of(queries, head_part(k_ref[...], index), allowed).astype(BF16)
        total += jnp.dot(probs, head_part(v_ref[...], index), preferred_element_type=F32)
    out_ref[...] = total.astype(BF16)


def attend_back_kernel(
    q_ref, k_ref, v_ref, g_ref, col_ref, row_ref, dq_ref, dk_ref, dv_ref, dk_sum, dv_sum
):
    step = pl.program_id(1)
    allowed = col_ref[...] == row_ref[...]
    queries = q_ref[...] * jnp.asarray(0.125, BF16)
    grads = g_ref[...]

    @pl.when(step == 0)
    def _():
        dk_sum[...] = jnp.zeros_like(dk_sum)
        dv_sum[...] = jnp.zeros_like(dv_sum)

    dq = jnp.zeros(dq_ref.shape, F32)
    for index in range(2):
        keys = head_part(k_ref[...], index)
        probs = probs_of(queries, keys, allowed)
        d_probs = matmul_nt(grads, head_part(v_ref[...], index))
        inner = jnp.sum(d_probs * probs, axis=-1, keepdims=True)
        scores_low = (probs * (d_probs - inner)).astype(BF16)
        dq += jnp.dot(scores_low, keys, preferred_element_type=F32)
        dk_sum[...] += matmul_tn(scores_low, head_part(queries, index))
        dv_sum[...] += matmul_tn(probs.astype(BF16), head_part(grads, index))
    dq_ref[...] = (dq * 0.125).astype(BF16)

    @pl.when(step == pl.num_programs(1) - 1)
    def _():
        dk_ref[...] = dk_sum[...].astype(BF16)
        dv_ref[...] = dv_sum[...].astype(BF16)


def attention_specs(length, pairs, block):
    rows = pl.BlockSpec((block, 128), lambda p, i: (i, p))

    def whole(third):
        return pl.BlockSpec((length, 128), lambda p, i: (0, p + third * pairs))

    labels = [
        pl.BlockSpec((block, 1), lambda p, i: (i, 0)),
        pl.BlockSpec((1, length), lambda p, i: (0, 0)),
    ]
    return rows, whole, labels


def attend(qkv, column, row):
    length = qkv.shape[0]
    width = qkv.shape[1] // 3
    pairs, block = width // 128, 256
    rows, whole, labels = attention_specs(length, pairs, block)
    return pl.pallas_call(
        attend_kernel,
        grid=(pairs, length // block),
        in_specs=[rows, whole(1), whole(2)] + labels,
        out_specs=rows,
        out_shape=jax.ShapeDtypeStruct((length, width), BF16),
        compiler_params=pltpu.CompilerParams(vmem_limit_bytes=40 << 20),
        cost_estimate=pl.CostEstimate(
            flops=60 * length * length * width, bytes_accessed=8 * length * width, transcendentals=0
        ),
    )(qkv, qkv, qkv, column, row)


def attend_back(qkv, grads, column, row, pair):
    length = qkv.shape[0]
    pairs, block = qkv.shape[1] // 384, 256
    labels = attention_specs(length, pairs, block)[2]
    out = jax.ShapeDtypeStruct((length, 128), BF16)

    def whole(third):
        return pl.BlockSpec((length, 128), lambda p, i: (0, pair + third * pairs))

    rows = pl.BlockSpec((block, 128), lambda p, i: (i, pair))
    kept = pl.BlockSpec((length, 128), lambda p, i: (0, 0))
    return pl.pallas_call(
        attend_back_kernel,
        grid=(1, length // block),
        in_specs=[rows, whole(1), whole(2), rows] + labels,
        out_specs=[pl.BlockSpec((block, 128), lambda p, i: (i, 0)), kept, kept],
        out_shape=[out, out, out],
        scratch_shapes=[pltpu.VMEM((length, 128), F32), pltpu.VMEM((length, 128), F32)],
        compiler_params=pltpu.CompilerParams(vmem_limit_bytes=48 << 20),
        cost_estimate=pl.CostEstimate(
            flops=95 * length * length * 128,
            bytes_accessed=14 * length * 128,
            transcendentals=0,
        ),
    )(qkv, qkv, qkv, grads, column, row)


def swap(stacked):
    count = stacked.shape[0]
    if count != 2:
        return lax.all_to_all(stacked, "ctx", 0, 0)
    place = lax.axis_index("ctx")
    mine = lax.dynamic_index_in_dim(stacked, place, 0, keepdims=False)
    sent = lax.dynamic_index_in_dim(stacked, 1 - place, 0, keepdims=False)
    got = lax.ppermute(sent, "ctx", [(0, 1), (1, 0)])
    first = place == 0
    return jnp.stack([jnp.where(first, mine, got), jnp.where(first, got, mine)])


def gather_ctx(array, count):
    if count != 2:
        return lax.all_gather(array, "ctx", axis=0, tiled=True)
    got = lax.ppermute(array, "ctx", [(0, 1), (1, 0)])
    first = lax.axis_index("ctx") == 0
    return jnp.concatenate([jnp.where(first, array, got), jnp.where(first, got, array)], axis=0)


def halve(array, dim, place, axis, pairs):
    mine = lax.dynamic_index_in_dim(array, place, dim, keepdims=False)
    sent = lax.dynamic_index_in_dim(array, 1 - place, dim, keepdims=False)
    got = lax.ppermute(sent, axis, pairs)
    return (mine.astype(F32) + got.astype(F32)).astype(BF16)


def sum_blocks(array, order):
    seq_count = array.shape[0]
    place = lax.axis_index("seq")
    deep = seq_count // 4
    array = array.reshape((deep, 2, 2) + array.shape[1:])
    left = ["z", "x", "core", "y"]
    for name in order:
        dim = left.index(name)
        if name == "core":
            pairs = [(i, i ^ 1) for i in range(seq_count)]
            array = halve(array, dim, lax.rem(place, 2), "seq", pairs)
        elif name == "x":
            pairs = [(i, i ^ 2) for i in range(seq_count)]
            array = halve(array, dim, lax.rem(place // 2, 2), "seq", pairs)
        else:
            array = halve(array, dim, lax.axis_index("ctx"), "ctx", [(0, 1), (1, 0)])
        left.remove(name)
    level = place // 4
    total = lax.dynamic_index_in_dim(array, level, 0, keepdims=False).astype(F32)
    for step in range(1, deep):
        sent = lax.dynamic_index_in_dim(array, lax.rem(level + step, deep), 0, keepdims=False)
        pairs = [(i, (i + 4 * step) % seq_count) for i in range(seq_count)]
        total += lax.ppermute(sent, "seq", pairs).astype(F32)
    return total


def sum_all(array, order):
    seq_count, ctx_count = lax.axis_size("seq"), lax.axis_size("ctx")
    if ctx_count != 2:
        return lax.psum_scatter(array, BOTH, scatter_dimension=0, tiled=False).astype(F32)
    return sum_blocks(array.reshape((seq_count, ctx_count) + array.shape[1:]), order)


def sum_seq(array):
    if lax.axis_size("ctx") != 2:
        return lax.psum_scatter(array, "seq", scatter_dimension=0, tiled=False)
    return sum_blocks(array, ("core", "x")).astype(BF16)


def split_sum(value):
    high = value.astype(BF16)
    return high, (value - high.astype(F32)).astype(BF16)


def per_device(
    tokens,
    segments,
    cotangent,
    w_query,
    b_query,
    w_key,
    w_value,
    b_value,
    w_output,
    b_output,
    gain_attn,
    shift_attn,
    w_inner,
    b_inner,
    w_outer,
    b_outer,
    gain_ffn,
    shift_ffn,
):
    rows, width = tokens.shape
    seq_count = lax.axis_size("seq")
    ctx_count = lax.axis_size("ctx")
    count = seq_count * ctx_count
    place = lax.axis_index("ctx")
    part = width // ctx_count
    own = w_query.shape[0]
    wide = b_inner.shape[0]
    labels = segments[0]
    column, row = labels[:, None], labels[None, :]

    vectors = jnp.concatenate(
        [b_query, b_value, b_output, gain_attn, shift_attn, b_outer, gain_ffn, shift_ffn, b_inner]
    )
    extra = jnp.pad(vectors[None, :], ((0, 15), (0, width - vectors.shape[0])))
    packed = jnp.concatenate([w_query, w_key, w_value, w_output, extra], axis=0)
    gathered = lax.all_gather(packed, BOTH, axis=0, tiled=False)
    tokens_all = gather_ctx(tokens, ctx_count)
    winner = lax.all_gather(w_inner, BOTH, axis=0, tiled=True)
    wouter = lax.all_gather(w_outer, BOTH, axis=0, tiled=True)

    wquery, wkey, wvalue, woutput = (
        gathered[:, i * own : (i + 1) * own].reshape(width, width) for i in range(4)
    )
    small = gathered[:, 4 * own].astype(F32)
    bquery, bvalue, boutput, gattn, sattn, bouter, gffn, sffn = (
        small[:, i * own : (i + 1) * own].reshape(width) for i in range(8)
    )
    binner = small[:, 8 * own : 8 * own + wide].reshape(-1)

    def my_cols(array):
        return lax.dynamic_slice_in_dim(array, place * part, part, array.ndim - 1)

    w_three = jnp.concatenate([my_cols(wquery), my_cols(wkey), my_cols(wvalue)], axis=1)
    b_three = jnp.concatenate([my_cols(bquery), jnp.zeros((part,), F32), my_cols(bvalue)])
    qkv = (jnp.dot(tokens_all, w_three, preferred_element_type=F32) + b_three).astype(BF16)
    mixed = attend(qkv, column, row)
    mixed = swap(mixed.reshape(ctx_count, rows, part))
    attended = jnp.transpose(mixed, (1, 0, 2)).reshape(rows, width)

    pre_one = (
        tokens.astype(F32) + jnp.dot(attended, woutput, preferred_element_type=F32) + boutput
    )
    normed_one = layer_norm(pre_one, gattn, sattn)
    normed_low = normed_one.astype(BF16)
    inner = jnp.dot(normed_low, winner, preferred_element_type=F32) + binner
    act_low = exact_gelu(inner).astype(BF16)
    pre_two = normed_one + jnp.dot(act_low, wouter, preferred_element_type=F32) + bouter
    out_value = layer_norm(pre_two, gffn, sffn)

    grad_out = cotangent.astype(F32)
    _, norm_two_back = jax.vjp(layer_norm, pre_two, gffn, sffn)
    d_pre_two, d_gain_two, d_shift_two = norm_two_back(grad_out)
    outer_low = d_pre_two.astype(BF16)
    grad_bouter = jnp.sum(outer_low.astype(F32), axis=0)
    part_wouter = matmul_tn(act_low, outer_low).astype(BF16)
    part_wouter = part_wouter.reshape(count, wide, width)
    d_act = matmul_nt(outer_low, wouter)
    _, gelu_back = jax.vjp(exact_gelu, inner)
    inner_low = gelu_back(d_act)[0].astype(BF16)
    grad_binner = jnp.sum(inner_low.astype(F32), axis=0)
    part_winner = matmul_tn(normed_low, inner_low).astype(BF16)
    part_winner = part_winner.reshape(count, own, wide * count)
    d_normed = d_pre_two + matmul_nt(inner_low, winner)

    _, norm_one_back = jax.vjp(layer_norm, pre_one, gattn, sattn)
    d_pre_one, d_gain_one, d_shift_one = norm_one_back(d_normed)
    out_low = d_pre_one.astype(BF16)
    grad_boutput = jnp.sum(out_low.astype(F32), axis=0)
    part_woutput = matmul_tn(attended, out_low).astype(BF16)
    sums = jnp.concatenate(
        [
            v.reshape(count, -1)
            for v in (
                grad_boutput, d_gain_one, d_shift_one, grad_bouter, d_gain_two, d_shift_two,
                grad_binner,
            )
        ],
        axis=1,
    )
    high, low = split_sum(sums)
    used = sums.shape[1]
    tail = jnp.pad(
        jnp.concatenate([high, low], axis=1)[:, None, :], ((0, 0), (0, 15), (0, width - 2 * used))
    )
    block = jnp.concatenate([part_woutput.reshape(count, own, width), tail], axis=1)
    out_low, part_wouter, part_winner, block = lax.optimization_barrier(
        (out_low, part_wouter, part_winner, block)
    )
    out_wouter = sum_all(part_wouter, ("core", "x", "y"))
    out_winner = sum_all(part_winner, ("core", "y", "x"))
    d_attended = matmul_nt(out_low, woutput).astype(BF16)
    d_mixed = swap(jnp.transpose(d_attended.reshape(rows, ctx_count, part), (1, 0, 2)))
    d_mixed = d_mixed.reshape(ctx_count * rows, part)

    block = sum_all(block, ("core", "y", "x"))
    out_woutput = block[:own].astype(F32)
    sums = (block[own, :used].astype(F32) + block[own, used : 2 * used].astype(F32))
    out_boutput, out_gattn, out_sattn, out_bouter, out_gffn, out_sffn = (
        sums[i * own : (i + 1) * own] for i in range(6)
    )
    out_binner = sums[6 * own :]

    backs = [attend_back(qkv, d_mixed, column, row, pair) for pair in range(part // 128)]
    d_three = jnp.concatenate([back[i] for i in range(3) for back in backs], axis=1)

    part_three = matmul_tn(tokens_all, d_three).astype(BF16)
    bias = jnp.sum(d_three.astype(F32), axis=0)

    def spread(vector):
        whole = jnp.zeros((width,), F32)
        whole = lax.dynamic_update_slice_in_dim(whole, vector, place * part, 0)
        return whole.reshape(seq_count, ctx_count, own)

    pair = jnp.concatenate([spread(bias[:part]), spread(bias[2 * part :])], axis=2)
    high, low = split_sum(pair)
    tail = jnp.pad(
        jnp.concatenate([high, low], axis=2)[:, :, None, :],
        ((0, 0), (0, 0), (0, 15), (0, 3 * part - 4 * own)),
    )
    block = jnp.concatenate(
        [part_three.reshape(seq_count, ctx_count, own, 3 * part), tail], axis=2
    )
    block = sum_seq(block)

    d_part = matmul_nt(d_three, w_three)
    got = swap(d_part.astype(BF16).reshape(ctx_count, rows, width))
    grad_tokens = d_pre_one + jnp.sum(got.astype(F32), axis=0)

    block = swap(block).astype(F32)
    out_wquery, out_wkey, out_wvalue = (
        jnp.transpose(block[:, :own, i * part : (i + 1) * part], (1, 0, 2)).reshape(own, width)
        for i in range(3)
    )
    pair = jnp.sum(block[:, own], axis=0)
    pair = pair[: 2 * own] + pair[2 * own : 4 * own]
    out_bquery, out_bvalue = pair[:own], pair[own:]
    return (
        out_value.astype(BF16),
        grad_tokens,
        out_wquery,
        out_bquery,
        out_wkey,
        out_wvalue,
        out_bvalue,
        out_woutput,
        out_boutput,
        out_gattn,
        out_sattn,
        out_winner,
        out_binner,
        out_wouter,
        out_bouter,
        out_gffn,
        out_sffn,
    )


def solution(mesh):
    matrix, vector = P(BOTH, None), P(BOTH)
    return jax.shard_map(
        per_device,
        mesh=mesh,
        in_specs=(
            matrix, P("seq", None), matrix, matrix, vector, matrix, matrix, vector, matrix,
            vector, vector, vector, matrix, vector, matrix, vector, vector, vector,
        ),
        out_specs=(
            matrix, matrix, matrix, vector, matrix, matrix, vector, matrix, vector, vector,
            vector, matrix, vector, matrix, vector, vector, vector,
        ),
        check_vma=False,
    )
```
